512 devices in a mesh: mesh: 128 (over y, z, core), sect: 4 (over x).
Axes of the slice: x: 4, y: 8, z: 8, core: 2. Of those that a mesh axis runs over, the one named last changes fastest.
Arguments:
- latent: bfloat16 [65536, 512], P('mesh', 'sect'), may hold values from -6 to 6
- export_rows: int32 [128, 32], P('mesh'), may hold values from 0 to 511, as said below
- halo_slots: int32 [128, 128, 8], P('mesh'), may hold values from 0 to 31
- tile_src: int32 [512, 16], P('mesh'), may hold values from 0 to 11, as said below
- tile_weight: bfloat16 [512, 16, 128, 128], P('mesh'), may hold values from -0.25 to 0.25
- send_w1: bfloat16 [512, 512], replicated, may hold values from -0.25 to 0.25
- send_b1: float32 [512], replicated, may hold values from -3 to 3
- send_w2: bfloat16 [512, 512], P(None, 'sect'), may hold values from -0.25 to 0.25
- send_b2: float32 [512], P('sect'), may hold values from -3 to 3
- node_w1: bfloat16 [1024, 512], replicated, may hold values from -0.1875 to 0.1875
- node_b1: float32 [512], replicated, may hold values from -3 to 3
- node_w2: bfloat16 [512, 512], P(None, 'sect')
- node_b2: bfloat16 [512], P('sect'), may hold values from -3 to 3
- ln_gain: float32 [512], P('sect'), may hold values from 0.5 to 1.5
- ln_bias: float32 [512], P('sect'), may hold values from -3 to 3
Outputs:
- updated: bfloat16 [65536, 512], P('mesh', 'sect')
The draws below stay inside these ranges and needn't reach their ends.
Inputs may be any that keep to these rules, and one draw needn't show every extreme that they name: `export_rows`: the 32 rows listed for one mesh index are distinct local row numbers of that index. `halo_slots`: each entry names a position in the offered list of mesh index j; repeats may occur. `tile_src`: among the tiles of one mesh index's 4 blocks, every one of the 12 extended blocks is named at least once.
All inputs are finite; a program needn't handle non-finite values.
Results may differ from the reference program's by a relative error of at most 0.008.
Values may be sent and summed in bfloat16 or wider, within the bound.
No kernel may reach another device: no remote copies, remote signals or barrier semaphores. Data moves between devices by JAX's collectives and lax.ppermute only.
A program may use at most 64 MiB of HBM per device.

```python
import math
import jax
import jax.numpy as jnp
from jax import lax

D = 512
TB = 128
MB = 4
K = 16
HALO = 8
EXPORT = 32
MROWS = 512
MESH = 65536
MBLOCKS = 512
XBLK = 12
N_MESH = 128


def draw_export_rows(key, part):
    key = jax.random.fold_in(key, 5)
    keys = jax.random.split(key, N_MESH)
    picked = jax.vmap(lambda single: jax.random.permutation(single, MROWS)[:EXPORT])(keys)
    return picked.astype(jnp.int32)


def draw_tile_src(key, part):
    key = jax.random.fold_in(key, 11)

    def one_index(single):
        first, second, third = jax.random.split(single, 3)
        count = MB * K
        position = jnp.arange(count, dtype=jnp.int32)
        offset = jax.random.randint(first, (), 0, XBLK)
        cover = (position + offset) % XBLK
        extra = jax.random.randint(second, (count,), 0, XBLK)
        flat = jnp.where(position < XBLK, cover, extra)
        order = jax.random.permutation(third, count)
        return flat[order].reshape(MB, K)
    keys = jax.random.split(key, N_MESH)
    return jax.vmap(one_index)(keys).reshape(MBLOCKS, K).astype(jnp.int32)


def draw_node_w2(key, part):
    key = jax.random.fold_in(key, 7)
    first, second = jax.random.split(key)
    base = jax.random.normal(first, (D, D), jnp.float32)
    spread = jax.random.uniform(second, (D,), jnp.float32, math.log(0.5), math.log(2.0))
    ramp = jnp.exp(math.log(3.0) * jnp.arange(D, dtype=jnp.float32) / (D - 1))
    values = base * jnp.exp(spread) * ramp / math.sqrt(D)
    return values.astype(jnp.bfloat16)


def place_ends(result, key, low, high):
    dims = result.shape
    place = [jax.random.randint(jax.random.fold_in(key, axis), (), 0, dims[axis]) for axis in range(len(dims))]
    result = result.at[tuple(place)].set(low)
    longest = dims.index(max(dims))
    place[longest] = (place[longest] + 1) % dims[longest]
    return result.at[tuple(place)].set(high)


def block_levels(key, shape, cuts, least, high):
    level, own = 1.0, jax.random.fold_in(key, 6)
    for axis_at, shards_of in cuts:
        draws = jnp.exp(jax.random.uniform(jax.random.fold_in(own, axis_at), (shards_of,), jnp.float32, least / len(cuts), high / len(cuts)))
        level = level * jnp.repeat(draws, shape[axis_at] // shards_of).reshape([-1 if axis == axis_at else 1 for axis in range(len(shape))])
    return level


def gaussian(own_key, shape, scale, most, cuts=(), kind=jnp.bfloat16):
    result = jax.random.normal(own_key, shape, jnp.float32) * scale
    if len(cuts) > 0:
        result = block_levels(own_key, shape, cuts, -0.22, 0.18) * result
    return jnp.clip(result, min=-most, max=most).astype(kind)


def setup_inputs(seed: int = 0) -> dict:
    streams_of = jax.random.split(jax.random.key(seed), 16)
    return {
        "latent": gaussian(streams_of[0], (MESH, D), 1.0, 6.0, ((0, 128), (1, 4))),
        "export_rows": draw_export_rows(jax.random.fold_in(streams_of[15], 71), 0),
        "halo_slots": place_ends(jax.random.randint(streams_of[2], (N_MESH, N_MESH, HALO), 0, EXPORT), jax.random.fold_in(streams_of[2], 1), 0, EXPORT - 1).astype(jnp.int32),
        "tile_src": draw_tile_src(jax.random.fold_in(streams_of[15], 71), 0),
        "tile_weight": gaussian(streams_of[4], (MBLOCKS, K, TB, TB), (4 * TB) ** -0.5, 0.25, ((0, 128),)),
        "send_w1": gaussian(streams_of[5], (D, D), D ** -0.5, 0.25),
        "send_b1": gaussian(streams_of[6], (D,), 0.5, 3.0, (), jnp.float32),
        "send_w2": gaussian(streams_of[7], (D, D), D ** -0.5, 0.25, ((1, 4),)),
        "send_b2": gaussian(streams_of[8], (D,), 0.5, 3.0, ((0, 4),), jnp.float32),
        "node_w1": gaussian(streams_of[9], (2 * D, D), (2 * D) ** -0.5, 0.1875),
        "node_b1": gaussian(streams_of[10], (D,), 0.5, 3.0, (), jnp.float32),
        "node_w2": draw_node_w2(jax.random.fold_in(streams_of[15], 71), 0),
        "node_b2": gaussian(streams_of[12], (D,), 0.5, 3.0, ((0, 4),)),
        "ln_gain": jnp.clip(1.0 + 0.1 * jax.random.normal(streams_of[13], (D,), jnp.float32), 0.5, 1.5),
        "ln_bias": gaussian(streams_of[14], (D,), 0.5, 3.0, ((0, 4),), jnp.float32),
    }


def reference(latent, export_rows, halo_slots, tile_src, tile_weight, send_w1, send_b1, send_w2, send_b2, node_w1, node_b1, node_w2, node_b2, ln_gain, ln_bias):
    hidden_send = jax.nn.silu(jnp.dot(latent, send_w1, preferred_element_type=jnp.float32) + send_b1).astype(jnp.bfloat16)
    message = (jnp.dot(hidden_send, send_w2, preferred_element_type=jnp.float32) + send_b2).astype(jnp.bfloat16)
    by_index = message.reshape(N_MESH, MROWS, D)
    offered = jnp.take_along_axis(by_index, export_rows[:, :, None].astype(jnp.int32), axis=1)
    peers = jnp.arange(N_MESH, dtype=jnp.int32)
    padding = XBLK * TB - MROWS - N_MESH * HALO

    def one_index(item):
        own, slots, sources, weights = item
        halo = offered[peers[:, None], slots].reshape(N_MESH * HALO, D)
        extended = jnp.concatenate([own, halo, jnp.zeros((padding, D), own.dtype)], 0).reshape(XBLK, TB, D)
        senders = extended[sources]
        summed = jnp.einsum('bkij,bkjc->bic', weights.astype(jnp.float32), senders.astype(jnp.float32))
        return summed.reshape(MROWS, D).astype(jnp.bfloat16)
    aggregate = lax.map(one_index, (by_index, halo_slots, tile_src.reshape(N_MESH, MB, K), tile_weight.reshape(N_MESH, MB, K, TB, TB)))
    aggregate = aggregate.reshape(N_MESH * MROWS, D)
    node_pre = jnp.dot(latent, node_w1[:D], preferred_element_type=jnp.float32) + jnp.dot(aggregate, node_w1[D:], preferred_element_type=jnp.float32) + node_b1
    node_hidden = jax.nn.silu(node_pre).astype(jnp.bfloat16)
    node_out = jnp.dot(node_hidden, node_w2, preferred_element_type=jnp.float32) + node_b2.astype(jnp.float32)
    mean = lax.optimization_barrier(jnp.mean(node_out, -1, keepdims=True))
    var = lax.optimization_barrier(jnp.mean(node_out * node_out, -1, keepdims=True)) - mean * mean
    normed = (node_out - mean) * lax.rsqrt(var + 1e-05)
    return (latent.astype(jnp.float32) + ln_gain * normed + ln_bias).astype(jnp.bfloat16)
```

```python
import jax
import jax.numpy as jnp
from jax import lax
from jax.sharding import Mesh
from jax.sharding import PartitionSpec as P

NODE = ("y", "z", "core")
EPS = 1e-05


def send(rows, w1, b1, w2, b2):
    hidden = jnp.dot(rows, w1, preferred_element_type=jnp.float32) + b1
    hidden = jax.nn.silu(hidden).astype(jnp.bfloat16)
    return (jnp.dot(hidden, w2, preferred_element_type=jnp.float32) + b2).astype(jnp.bfloat16)


def pick(index, rows):
    chosen = index[:, None] == jnp.arange(rows.shape[0], dtype=jnp.int32)[None, :]
    chosen = chosen.astype(jnp.bfloat16)
    return jnp.dot(chosen, rows, preferred_element_type=jnp.float32).astype(jnp.bfloat16)


def copies(block, axis):
    peers = lax.axis_size(axis)
    block = jnp.broadcast_to(block[None], (peers,) + block.shape)
    return lax.all_to_all(block, axis, 0, 0)


def local(
    latent,
    export_rows,
    halo_slots,
    tile_src,
    tile_weight,
    send_w1,
    send_b1,
    send_w2,
    send_b2,
    node_w1,
    node_b1,
    node_w2,
    node_b2,
    ln_gain,
    ln_bias,
):
    rows, share = latent.shape
    width = send_w1.shape[0]
    offers = export_rows.shape[1]
    takes = halo_slots.shape[2]
    n_y, n_z, n_core = (lax.axis_size(name) for name in NODE)
    layer = n_z * n_core

    offered_latent = pick(export_rows[0], latent)
    offered_latent = lax.all_gather(offered_latent, "sect", axis=1, tiled=True)
    offered = send(offered_latent, send_w1, send_b1, send_w2, send_b2)
    offered = lax.all_gather(offered, "core", axis=0, tiled=True)
    offered = copies(offered, "z").reshape(layer * offers, share)

    wanted = lax.all_to_all(halo_slots.reshape(n_y, layer * takes), "y", 0, 0, tiled=True)
    wanted = wanted + (jnp.arange(layer * takes, dtype=jnp.int32) // takes * offers)[None, :]
    halo = pick(wanted.reshape(-1), offered)
    halo = lax.all_to_all(halo, "y", 0, 0, tiled=True)

    whole_latent = copies(latent, "sect")
    whole_latent = jnp.concatenate([whole_latent[s] for s in range(width // share)], 1)
    tail = jnp.broadcast_to(node_b2[None], (16, share))
    whole_w2 = copies(jnp.concatenate([node_w2, tail], 0), "sect")
    whole_w2 = jnp.concatenate([whole_w2[s] for s in range(width // share)], 1)
    whole_w2, whole_b2 = whole_w2[:width], whole_w2[width]

    message = send(whole_latent, send_w1, send_b1, send_w2, send_b2)
    tile = tile_weight.shape[-1]
    used = rows + halo.shape[0]
    blocks = (used + tile - 1) // tile
    extended = jnp.concatenate(
        [message, halo, jnp.zeros((blocks * tile - used, share), jnp.bfloat16)], 0
    )
    extended = extended.reshape(blocks, tile, share)
    senders = extended[tile_src]
    summed = jnp.einsum("bkij,bkjc->bic", tile_weight, senders, preferred_element_type=jnp.float32)
    aggregate = summed.reshape(rows, share).astype(jnp.bfloat16)
    whole_aggregate = lax.all_gather(aggregate, "sect", axis=1, tiled=True)

    node_pre = jnp.dot(whole_latent, node_w1[:width], preferred_element_type=jnp.float32)
    node_pre = (
        node_pre
        + jnp.dot(whole_aggregate, node_w1[width:], preferred_element_type=jnp.float32)
        + node_b1
    )
    node_hidden = jax.nn.silu(node_pre).astype(jnp.bfloat16)
    whole_out = jnp.dot(node_hidden, whole_w2, preferred_element_type=jnp.float32)
    whole_out = whole_out + whole_b2.astype(jnp.float32)
    mean = jnp.mean(whole_out, -1, keepdims=True)
    var = jnp.mean(whole_out * whole_out, -1, keepdims=True) - mean * mean
    node_out = jnp.dot(node_hidden, node_w2, preferred_element_type=jnp.float32)
    node_out = node_out + node_b2.astype(jnp.float32)
    normed = (node_out - mean) * lax.rsqrt(var + EPS)
    return (latent.astype(jnp.float32) + ln_gain * normed + ln_bias).astype(jnp.bfloat16)


def solution(mesh):
    n_mesh, n_sect = mesh.devices.shape
    n_y = n_z = int(round((n_mesh // 2) ** 0.5))
    grid = Mesh(mesh.devices.reshape(n_y, n_z, 2, n_sect), NODE + ("sect",))
    in_specs = (
        P(NODE, "sect"),
        P(NODE, None),
        P(NODE, None, None),
        P(NODE, None),
        P(NODE, None, None, None),
        P(),
        P(),
        P(None, "sect"),
        P("sect"),
        P(),
        P(),
        P(None, "sect"),
        P("sect"),
        P("sect"),
        P("sect"),
    )
    out_specs = P(NODE, "sect")
    return jax.shard_map(local, mesh=grid, in_specs=in_specs, out_specs=out_specs, check_vma=False)
```

```python
import jax
import jax.numpy as jnp
from jax import lax
from jax.experimental import pallas as pl
from jax.experimental.pallas import tpu as pltpu
from jax.sharding import Mesh
from jax.sharding import PartitionSpec as P

NODE = ("y", "z", "core")
EPS = 1e-05
TAIL = 16

LIMIT = 60 << 20
WEIGHT = 10**10
bf16, f32, i32 = jnp.bfloat16, jnp.float32, jnp.int32


def call(body, operands, outs, scratch=(), scalars=(), part={}, flops=0, moved=0):
    count = len(operands)
    space = [pltpu.SMEM if i in scalars else pltpu.VMEM for i in range(count)]

    def kernel(*refs):
        sources, rest = refs[:count], refs[count:]
        results, held, rest = rest[: len(outs)], rest[len(outs) :][:count], rest[len(outs) + count :]
        sems, extra = rest[-1], rest[:-1]
        copies = [
            pltpu.make_async_copy(
                source.at[pl.ds(*part[i])] if i in part else source, target, sems.at[i]
            )
            for i, (source, target) in enumerate(zip(sources, held))
        ]
        for copy in copies:
            copy.start()

        def ready(i):
            def get():
                if copies[i] is not None:
                    copies[i].wait()
                    copies[i] = None
                return held[i]

            return get

        gets = [ready(i) for i in range(count)]
        body(*gets, *results, *extra)
        for get in gets:
            get()

    return pl.pallas_call(
        kernel,
        out_shape=[jax.ShapeDtypeStruct(shape, kind) for shape, kind in outs],
        in_specs=[pl.BlockSpec(memory_space=pltpu.HBM)] * count,
        out_specs=[pl.BlockSpec(memory_space=pltpu.VMEM)] * len(outs),
        scratch_shapes=[
            kind((part[i][1],) + v.shape[1:] if i in part else v.shape, v.dtype)
            for i, (kind, v) in enumerate(zip(space, operands))
        ]
        + list(scratch)
        + [pltpu.SemaphoreType.DMA((count,))],
        compiler_params=pltpu.CompilerParams(vmem_limit_bytes=LIMIT),
        cost_estimate=pl.CostEstimate(flops=flops, bytes_accessed=moved, transcendentals=0),
        name=body.__name__,
    )(*operands)


def matmul(left, right):
    return jnp.dot(left, right, preferred_element_type=f32)


def silu(value):
    half = 0.5 * value
    return half + half * jnp.tanh(half)


def pack(export, latent, slots, offered, wanted, wide):
    rows, offers = latent().shape[0], offered.shape[0]
    wide[pl.ds(0, rows), :] = latent()[...].astype(f32)
    chosen = export()
    for e in range(offers):
        wide[pl.ds(rows + e, 1), :] = wide[pl.ds(chosen[0, e], 1), :]
    offered[...] = wide[pl.ds(rows, offers), :].astype(bf16)
    for peer in range(wanted.shape[0]):
        wanted[peer] = slots()[...]


def offer(gathered, w1, b1, w2, b2, out):
    offers = out.shape[1]
    parts = gathered().shape[0] // offers
    rows = jnp.concatenate([gathered()[pl.ds(p * offers, offers), :] for p in range(parts)], 1)
    hidden = silu(matmul(rows, w1()[...]) + b1()[...]).astype(bf16)
    message = (matmul(hidden, w2()[...]) + b2()[...]).astype(bf16)
    for peer in range(out.shape[0]):
        out[peer] = message


def bundle(latent, w2, b2, side):
    rows = latent().shape[0]
    side[pl.ds(0, rows), :] = latent()[...]
    side[pl.ds(rows, rows), :] = w2()[...]
    row = b2()[...].astype(f32)
    side[pl.ds(2 * rows, TAIL), :] = jnp.broadcast_to(row, (TAIL, row.shape[1])).astype(bf16)


def select(wanted, offered, out):
    wanted, offered = wanted(), offered()
    n_y, takes, lanes = wanted.shape
    layer = lanes // n_y
    n_z = layer // 2
    offers = offered.shape[0] // layer
    quad = 128 // offers
    half = offered.shape[0] // 2
    shift = lax.rem(lanes - lax.axis_index("y") * layer, lanes)
    lane = lax.broadcasted_iota(i32, (takes, 128), 1)
    blank = jnp.zeros((takes, 128), f32)
    for q in range(n_z // quad):
        sources = jnp.concatenate(
            [offered[pl.ds(c * half + q * 128, 128), :] for c in range(2)], 0
        )
        chosen = []
        for peer in range(n_y):
            table = pltpu.roll(wanted[peer], shift, 1)
            for part in range(quad):
                z = q * quad + part
                first, second = [
                    jnp.where(
                        table[:, 2 * z + c : 2 * z + c + 1] + part * offers == lane, 1.0, 0.0
                    )
                    for c in range(2)
                ]
                chosen.append(jnp.concatenate([first, blank], 1))
                chosen.append(jnp.concatenate([blank, second], 1))
        chosen = jnp.concatenate(chosen, 0).astype(bf16)
        rows = matmul(chosen, sources).astype(bf16)
        depth = quad * 2 * takes
        for peer in range(n_y):
            out[peer, pl.ds(q * depth, depth), :] = rows[peer * depth : (peer + 1) * depth]


def send(side0, side1, side2, side3, w1, b1, w2, b2, upper_w, message, upper):
    rows, share = message.shape
    width = upper.shape[1]
    sides = [side() for side in (side0, side1, side2, side3)]
    parts = len(sides)
    here = lax.axis_index("sect")
    order = [lax.rem(here + parts - k, parts) * share for k in range(parts)]

    def rolled(values):
        return jnp.concatenate([values[pl.ds(pl.multiple_of(o, share), share), :] for o in order], 0)

    step = rows // 2
    for turn in range(2):
        now = rolled(w1() if turn == 0 else upper_w())
        for r in range(0, rows, step):
            at = pl.ds(r, step)
            x = jnp.concatenate([side[at, :] for side in sides], 1)
            if turn == 0:
                hidden = silu(matmul(x, now) + b1()[...]).astype(bf16)
                message[at, :] = (matmul(hidden, w2()[...]) + b2()[...]).astype(bf16)
            else:
                upper[at, :] = matmul(x, now)


def tiles(source, message, halo, weight, out, extended):
    tile, share = extended.shape[1:]
    own = message().shape[0] // tile
    for b in range(own):
        extended[b] = message()[pl.ds(b * tile, tile), :]
    for b in range(halo().shape[0]):
        extended[own + b] = halo()[b]
    src = source()
    blocks, terms = src.shape
    group = 4
    for b in range(blocks):
        total = jnp.zeros((tile, share), f32)
        for k in range(0, terms, group):
            left = jnp.concatenate([weight()[b, k + g] for g in range(group)], 1)
            right = jnp.concatenate([extended[src[b, k + g]] for g in range(group)], 0)
            total = total + matmul(left, right)
        total = total.astype(bf16)
        for peer in range(out.shape[0]):
            out[peer, pl.ds(b * tile, tile), :] = total


def node(aggregate, lower_w, upper, b1, side0, side1, side2, side3, gain, bias, out):
    parts, rows, share = aggregate().shape
    sides = [side() for side in (side0, side1, side2, side3)]
    w2 = jnp.concatenate([side[pl.ds(rows, rows), :] for side in sides], 1)
    b2 = jnp.concatenate([side[pl.ds(2 * rows, 1), :] for side in sides], 1).astype(f32)
    width = share * parts
    step = rows // 2
    for r in range(0, rows, step):
        at = pl.ds(r, step)
        x = jnp.concatenate([aggregate()[p, at, :] for p in range(parts)], 1)
        hidden = silu(upper()[at, :] + matmul(x, lower_w()[...]) + b1()[...]).astype(bf16)
        every = matmul(hidden, w2) + b2
        split = [every[:, p * share : (p + 1) * share] for p in range(parts)]
        mine = split[0]
        total = jnp.sum(sum(split), 1, keepdims=True)
        squares = jnp.sum(sum(v * v for v in split), 1, keepdims=True)
        mean = total * (1.0 / width)
        var = squares * (1.0 / width) - mean * mean
        normed = (mine - mean) * lax.rsqrt(var + EPS)
        latent = sides[0][at, :].astype(f32)
        out[at, :] = (latent + gain()[...] * normed + bias()[...]).astype(bf16)


def local(
    latent,
    export_rows,
    halo_slots,
    tile_src,
    tile_weight,
    send_w1,
    send_b1,
    send_w2,
    send_b2,
    node_w1,
    node_b1,
    node_w2,
    node_b2,
    ln_gain,
    ln_bias,
):
    rows, share = latent.shape
    width = send_w1.shape[0]
    offers = export_rows.shape[1]
    takes = halo_slots.shape[2]
    n_y, n_z, n_core, n_sect = (lax.axis_size(name) for name in NODE + ("sect",))
    layer = n_z * n_core
    tile = tile_weight.shape[-1]
    send_b1, send_b2, node_b1, node_b2, ln_gain, ln_bias = (
        v[None] for v in (send_b1, send_b2, node_b1, node_b2, ln_gain, ln_bias)
    )

    sender = (send_w1, send_b1, send_w2, send_b2)
    slots = jnp.swapaxes(halo_slots[0], 0, 1)
    offered, wanted = call(
        pack,
        (export_rows, latent, slots),
        [((offers, share), bf16), ((n_y, takes, n_y * layer), i32)],
        [pltpu.VMEM((rows + offers, share), f32)],
        scalars=(0,),
    )

    wanted = lax.all_to_all(wanted, "y", 0, 0)
    for pairs in ([[0, 1], [2, 3]], [[0, 3], [1, 2]]):
        offered = lax.all_gather(offered, "sect", axis=0, tiled=True, axis_index_groups=pairs)
    offered, wanted = lax.optimization_barrier((offered, wanted))
    (offered,) = call(offer, (offered, *sender), [((n_z, offers, share), bf16)])

    offered, latent, node_w2, node_b2 = lax.optimization_barrier(
        (offered, latent, node_w2, node_b2)
    )
    offered = lax.all_to_all(offered, "z", 0, 0).reshape(n_z * offers, share)
    (side,) = call(
        bundle,
        (latent, node_w2, node_b2),
        [((2 * rows + TAIL, share), bf16)],
        flops=WEIGHT,
        moved=4 * rows * share,
    )
    sides = [side] + [
        lax.ppermute(side, "sect", [(i, (i + k) % n_sect) for i in range(n_sect)])
        for k in range(1, n_sect)
    ]
    offered = lax.all_gather(offered, "core", axis=0, tiled=True)
    (halo,) = call(
        select,
        (wanted, offered),
        [((n_y, layer * takes, share), bf16)],
        flops=2 * WEIGHT,
    )

    halo, *sides = lax.optimization_barrier((halo, *sides))
    halo = lax.all_to_all(halo, "y", 0, 0)
    message, upper = call(
        send,
        (*sides, *sender, node_w1),
        [((rows, share), bf16), ((rows, width), f32)],
        part={8: (0, width)},
        flops=2 * rows * width * (2 * width + share),
        moved=4 * rows * width,
    )

    (aggregate,) = call(
        tiles,
        (tile_src, message, halo, tile_weight),
        [((n_sect, rows, share), bf16)],
        [pltpu.VMEM((rows // tile + n_y, tile, share), bf16)],
        scalars=(0,),
    )
    aggregate = lax.all_to_all(aggregate, "sect", 0, 0)

    (updated,) = call(
        node,
        (aggregate, node_w1, upper, node_b1, *sides, ln_gain, ln_bias),
        [((rows, share), bf16)],
        part={1: (width, width)},
    )
    return updated


def solution(mesh):
    n_mesh, n_sect = mesh.devices.shape
    n_y = n_z = int(round((n_mesh // 2) ** 0.5))
    grid = Mesh(mesh.devices.reshape(n_y, n_z, 2, n_sect), NODE + ("sect",))
    in_specs = (
        P(NODE, "sect"),
        P(NODE, None),
        P(NODE, None, None),
        P(NODE, None),
        P(NODE, None, None, None),
        P(),
        P(),
        P(None, "sect"),
        P("sect"),
        P(),
        P(),
        P(None, "sect"),
        P("sect"),
        P("sect"),
        P("sect"),
    )
    out_specs = P(NODE, "sect")
    return jax.shard_map(local, mesh=grid, in_specs=in_specs, out_specs=out_specs, check_vma=False)
```

```python
import jax
import jax.numpy as jnp
from jax import lax
from jax.experimental import pallas as pl
from jax.experimental.pallas import tpu as pltpu
from jax.sharding import Mesh
from jax.sharding import PartitionSpec as P

NODE = ("y", "z", "core")
EPS = 1e-05
TAIL = 16

LIMIT = 60 << 20
ROOM = 40 << 20
WEIGHT = 10**10
bf16, f32, i32 = jnp.bfloat16, jnp.float32, jnp.int32


def call(body, operands, outs, scratch=(), scalars=(), part={}, flops=0, moved=0, limit=LIMIT):
    count = len(operands)
    space = [pltpu.SMEM if i in scalars else pltpu.VMEM for i in range(count)]

    def kernel(*refs):
        sources, rest = refs[:count], refs[count:]
        results, held, rest = rest[: len(outs)], rest[len(outs) :][:count], rest[len(outs) + count :]
        sems, extra = rest[-1], rest[:-1]
        copies = [
            pltpu.make_async_copy(
                source.at[part[i][0]] if i in part else source, target, sems.at[i]
            )
            for i, (source, target) in enumerate(zip(sources, held))
        ]
        for copy in copies:
            copy.start()

        def ready(i):
            def get():
                if copies[i] is not None:
                    copies[i].wait()
                    copies[i] = None
                return held[i]

            return get

        gets = [ready(i) for i in range(count)]
        body(*gets, *results, *extra)
        for get in gets:
            get()

    return pl.pallas_call(
        kernel,
        out_shape=[jax.ShapeDtypeStruct(shape, kind) for shape, kind in outs],
        in_specs=[pl.BlockSpec(memory_space=pltpu.HBM)] * count,
        out_specs=[pl.BlockSpec(memory_space=pltpu.VMEM)] * len(outs),
        scratch_shapes=[
            kind(part[i][1] if i in part else v.shape, v.dtype)
            for i, (kind, v) in enumerate(zip(space, operands))
        ]
        + list(scratch)
        + [pltpu.SemaphoreType.DMA((count,))],
        compiler_params=pltpu.CompilerParams(vmem_limit_bytes=limit),
        cost_estimate=pl.CostEstimate(flops=flops, bytes_accessed=moved, transcendentals=0),
        name=body.__name__,
    )(*operands)


def matmul(left, right):
    return jnp.dot(left, right, preferred_element_type=f32)


def silu(value):
    half = 0.5 * value
    return half + half * jnp.tanh(half)


def gather(block, beside=None):
    near, far = [[0, 1], [2, 3]], [[0, 3], [1, 2]]
    turned = [[0, 1], [3, 2]]
    for first, second in ((near, far), (far, turned)):
        groups = first + [[4 + i for i in group] for group in second]
        if block.ndim > 2 and beside is not None:
            block, beside = lax.optimization_barrier((block, beside))
        block = lax.all_gather(
            block, ("core", "sect"), axis=0, axis_index_groups=groups, tiled=block.ndim > 2
        )
    return block if beside is None else (block, beside)


def ordered(whole):
    core = lax.axis_index("core")
    return [whole.at[0], whole.at[1 + core], whole.at[2 + core], whole.at[3 - 2 * core]]


def offer(export, latent, w1, b1, w2, b2, out):
    rows = latent().shape[1]
    offers = out.shape[1]
    table = jnp.broadcast_to(export()[...].astype(f32), (offers, offers))
    on = lax.broadcasted_iota(i32, table.shape, 0) == lax.broadcasted_iota(i32, table.shape, 1)
    column = jnp.sum(jnp.where(on, table, 0.0), 1, keepdims=True).astype(i32)
    chosen = column == lax.broadcasted_iota(i32, (offers, rows), 1)
    chosen = jnp.where(chosen, 1.0, 0.0).astype(bf16)
    every = jnp.concatenate([part[...] for part in ordered(latent())], 1)
    picked = matmul(chosen, every).astype(bf16)
    hidden = silu(matmul(picked, w1()[...]) + b1()[...]).astype(bf16)
    message = (matmul(hidden, w2()[...]) + b2()[...]).astype(bf16)
    for peer in range(out.shape[0]):
        out[peer] = message


def select(wanted, offered, out):
    wanted, offered = wanted(), offered()
    n_z, takes, lanes = wanted.shape
    column = 2 * n_z
    n_y = lanes // column
    offers = offered.shape[0] // (2 * n_y)
    quad = 128 // offers
    half = offered.shape[0] // 2
    shift = lax.rem(lanes - 2 * lax.axis_index("z"), lanes)
    lane = lax.broadcasted_iota(i32, (takes, 128), 1)
    blank = jnp.zeros((takes, 128), f32)
    for q in range(n_y // quad):
        sources = jnp.concatenate(
            [offered[pl.ds(c * half + q * 128, 128), :] for c in range(2)], 0
        )
        chosen = []
        for peer in range(n_z):
            table = pltpu.roll(wanted[peer], shift, 1)
            for part in range(quad):
                at = (q * quad + part) * column
                first, second = [
                    jnp.where(
                        table[:, at + c : at + c + 1] + part * offers == lane, 1.0, 0.0
                    )
                    for c in range(2)
                ]
                chosen.append(jnp.concatenate([first, blank], 1))
                chosen.append(jnp.concatenate([blank, second], 1))
        chosen = jnp.concatenate(chosen, 0).astype(bf16)
        rows = matmul(chosen, sources).astype(bf16)
        depth = quad * 2 * takes
        for peer in range(n_z):
            out[peer, pl.ds(q * depth, depth), :] = rows[peer * depth : (peer + 1) * depth]


def send(latent, w1, b1, w2, b2, node_w2, node_b2, message, side):
    rows = latent().shape[1]
    blocks = ordered(latent())
    step = rows // 2
    for r in range(0, rows, step):
        at = pl.ds(r, step)
        x = jnp.concatenate([block[at, :] for block in blocks], 1)
        hidden = silu(matmul(x, w1()[...]) + b1()[...]).astype(bf16)
        message[at, :] = (matmul(hidden, w2()[...]) + b2()[...]).astype(bf16)
    width = node_w2().shape[0]
    side[pl.ds(0, width), :] = node_w2()[...]
    row = node_b2()[...].astype(f32)
    side[pl.ds(width, TAIL), :] = jnp.broadcast_to(row, (TAIL, row.shape[1])).astype(bf16)


def above(latent, weight, side0, side1, upper, pair):
    rows = latent().shape[1]
    blocks = ordered(latent())
    step = rows // 2
    for r in range(0, rows, step):
        at = pl.ds(r, step)
        x = jnp.concatenate([block[at, :] for block in blocks], 1)
        upper[at, :] = matmul(x, weight()[...])
    pair[0] = side0()[...]
    pair[1] = side1()[...]


def tiles(source, message, halo, *rest):
    *weight, out, extended = rest
    tile, share = extended.shape[1:]
    own = message().shape[0] // tile
    for b in range(own):
        extended[b] = message()[pl.ds(b * tile, tile), :]
    peers, rows, _ = halo().shape
    run = tile // peers
    for b in range(rows // run):
        for peer in range(peers):
            extended[own + b, pl.ds(peer * run, run), :] = halo()[peer, pl.ds(b * run, run), :]
    src = source()
    group = 4
    for b, block in enumerate(weight):
        terms = block().shape[0]
        total = jnp.zeros((tile, share), f32)
        for k in range(0, terms, group):
            left = jnp.concatenate([block()[k + g] for g in range(group)], 1)
            right = jnp.concatenate([extended[src[b, k + g]] for g in range(group)], 0)
            total = total + matmul(left, right)
        out[pl.ds(b * tile, tile), :] = total.astype(bf16)


def node(lower_w, b1, *rest):
    *chunks, pair0, pair1, latent, gain, bias, out = rest
    sides = []
    r = 0
    for aggregate, upper in zip(chunks[::2], chunks[1::2]):
        parts, step, share = aggregate().shape
        width = share * parts
        at = pl.ds(r, step)
        r += step
        x = jnp.concatenate([part[...] for part in ordered(aggregate())], 1)
        hidden = silu(upper()[...] + matmul(x, lower_w()[...]) + b1()[...]).astype(bf16)
        if not sides:
            sides = [pair()[p] for pair in (pair0, pair1) for p in range(2)]
            w2 = jnp.concatenate([side[:width] for side in sides], 1)
            b2 = jnp.concatenate([side[width : width + 1] for side in sides], 1).astype(f32)
        every = matmul(hidden, w2) + b2
        split = [every[:, p * share : (p + 1) * share] for p in range(parts)]
        mine = split[0]
        total = jnp.sum(sum(split), 1, keepdims=True)
        squares = jnp.sum(sum(v * v for v in split), 1, keepdims=True)
        mean = total * (1.0 / width)
        var = squares * (1.0 / width) - mean * mean
        normed = (mine - mean) * lax.rsqrt(var + EPS)
        result = latent()[at, :].astype(f32) + gain()[...] * normed + bias()[...]
        out[at, :] = result.astype(bf16)


def local(
    latent,
    export_rows,
    halo_slots,
    tile_src,
    tile_weight,
    send_w1,
    send_b1,
    send_w2,
    send_b2,
    node_w1,
    node_b1,
    node_w2,
    node_b2,
    ln_gain,
    ln_bias,
):
    rows, share = latent.shape
    width = send_w1.shape[0]
    offers = export_rows.shape[1]
    takes = halo_slots.shape[2]
    n_y, n_z, n_core, n_sect = (lax.axis_size(name) for name in NODE + ("sect",))
    tile = tile_weight.shape[-1]
    send_b1, send_b2, node_b1, node_b2, ln_gain, ln_bias = (
        v[None] for v in (send_b1, send_b2, node_b1, node_b2, ln_gain, ln_bias)
    )

    sender = (send_w1, send_b1, send_w2, send_b2)

    slots = jnp.swapaxes(halo_slots[0], 0, 1)
    wanted = lax.all_to_all(jnp.broadcast_to(slots[None], (n_z,) + slots.shape), "z", 0, 0)
    whole = gather(latent)
    whole, wanted = lax.optimization_barrier((whole, wanted))
    (offered,) = call(
        offer, (export_rows, whole, *sender), [((n_y, offers, share), bf16)]
    )

    offered, later = lax.optimization_barrier((offered, whole))
    offered = lax.all_to_all(offered, "y", 0, 0).reshape(n_y * offers, share)
    message, side = call(
        send,
        (later, *sender, node_w2, node_b2),
        [((rows, share), bf16), ((width + TAIL, share), bf16)],
        flops=WEIGHT,
    )
    other = lax.ppermute(side, "sect", [(i, i ^ 1) for i in range(n_sect)])
    offered = lax.all_gather(offered, "core", axis=0, tiled=True)
    (halo,) = call(
        select,
        (wanted, offered),
        [((n_z, n_y * n_core * takes, share), bf16)],
        flops=2 * WEIGHT,
        limit=ROOM,
    )

    halo, other, later = lax.optimization_barrier((halo, other, later))
    halo = lax.all_to_all(halo, "z", 0, 0)
    upper, pair = call(
        above,
        (later, node_w1, side, other),
        [((rows, width), f32), ((2, width + TAIL, share), bf16)],
        part={1: (pl.ds(0, width), (width, width))},
        flops=WEIGHT,
    )
    others = lax.ppermute(pair, "sect", [(i, n_sect - 1 - i) for i in range(n_sect)])

    blocks, terms = tile_src.shape
    (aggregate,) = call(
        tiles,
        (tile_src, message, halo) + (tile_weight,) * blocks,
        [((rows, share), bf16)],
        [pltpu.VMEM((rows // tile + n_y, tile, share), bf16)],
        scalars=(0,),
        part={3 + b: (b, (terms, tile, tile)) for b in range(blocks)},
        limit=ROOM,
        flops=2 * WEIGHT,
    )
    aggregate, others = gather(aggregate, others)

    step = rows // 2
    part = {0: (pl.ds(width, width), (width, width))}
    for c in range(2):
        at = pl.ds(c * step, step)
        part[2 + 2 * c] = ((slice(None), at), (n_sect, step, share))
        part[3 + 2 * c] = (at, (step, width))
    (updated,) = call(
        node,
        (node_w1, node_b1)
        + (aggregate, upper) * 2
        + (pair, others, latent, ln_gain, ln_bias),
        [((rows, share), bf16)],
        part=part,
        limit=ROOM,
    )
    return updated


def solution(mesh):
    n_mesh, n_sect = mesh.devices.shape
    n_y = n_z = int(round((n_mesh // 2) ** 0.5))
    grid = Mesh(mesh.devices.reshape(n_y, n_z, 2, n_sect), NODE + ("sect",))
    in_specs = (
        P(NODE, "sect"),
        P(NODE, None),
        P(NODE, None, None),
        P(NODE, None),
        P(NODE, None, None, None),
        P(),
        P(),
        P(None, "sect"),
        P("sect"),
        P(),
        P(),
        P(None, "sect"),
        P("sect"),
        P("sect"),
        P("sect"),
    )
    out_specs = P(NODE, "sect")
    return jax.shard_map(local, mesh=grid, in_specs=in_specs, out_specs=out_specs, check_vma=False)
```

```python
import jax
import jax.numpy as jnp
from jax import lax
from jax.experimental import pallas as pl
from jax.experimental.pallas import tpu as pltpu
from jax.sharding import Mesh
from jax.sharding import PartitionSpec as P

NODE = ("y", "z", "core")
EPS = 1e-05
TAIL = 16

LIMIT = 60 << 20
ROOM = 40 << 20
WEIGHT = 10**10
bf16, f32, i32 = jnp.bfloat16, jnp.float32, jnp.int32


def call(body, operands, outs, scratch=(), scalars=(), part={}, flops=0, moved=0, limit=LIMIT):
    count = len(operands)
    space = [pltpu.SMEM if i in scalars else pltpu.VMEM for i in range(count)]

    def kernel(*refs):
        sources, rest = refs[:count], refs[count:]
        results, held, rest = rest[: len(outs)], rest[len(outs) :][:count], rest[len(outs) + count :]
        sems, extra = rest[-1], rest[:-1]
        copies = [
            pltpu.make_async_copy(
                source.at[part[i][0]] if i in part else source, target, sems.at[i]
            )
            for i, (source, target) in enumerate(zip(sources, held))
        ]
        for copy in copies:
            copy.start()

        def ready(i):
            def get():
                if copies[i] is not None:
                    copies[i].wait()
                    copies[i] = None
                return held[i]

            return get

        gets = [ready(i) for i in range(count)]
        body(*gets, *results, *extra)
        for get in gets:
            get()

    return pl.pallas_call(
        kernel,
        out_shape=[jax.ShapeDtypeStruct(shape, kind) for shape, kind in outs],
        in_specs=[pl.BlockSpec(memory_space=pltpu.HBM)] * count,
        out_specs=[pl.BlockSpec(memory_space=pltpu.VMEM)] * len(outs),
        scratch_shapes=[
            kind(part[i][1] if i in part else v.shape, v.dtype)
            for i, (kind, v) in enumerate(zip(space, operands))
        ]
        + list(scratch)
        + [pltpu.SemaphoreType.DMA((count,))],
        compiler_params=pltpu.CompilerParams(vmem_limit_bytes=limit),
        cost_estimate=pl.CostEstimate(flops=flops, bytes_accessed=moved, transcendentals=0),
        name=body.__name__,
    )(*operands)


def matmul(left, right):
    return jnp.dot(left, right, preferred_element_type=f32)


def silu(value):
    half = 0.5 * value
    return half + half * jnp.tanh(half)


def gather(block, beside=None):
    near, far = [[0, 1], [2, 3]], [[0, 3], [1, 2]]
    turned = [[0, 1], [3, 2]]
    for first, second in ((near, far), (far, turned)):
        groups = first + [[4 + i for i in group] for group in second]
        if block.ndim > 2 and beside is not None:
            block, beside = lax.optimization_barrier((block, beside))
        block = lax.all_gather(
            block, ("core", "sect"), axis=0, axis_index_groups=groups, tiled=block.ndim > 2
        )
    return block if beside is None else (block, beside)


def ordered(whole):
    core = lax.axis_index("core")
    return [whole.at[0], whole.at[1 + core], whole.at[2 + core], whole.at[3 - 2 * core]]


def offer(export, latent, w1, b1, w2, b2, out):
    rows = latent().shape[1]
    offers = out.shape[1]
    table = jnp.broadcast_to(export()[...].astype(f32), (offers, offers))
    on = lax.broadcasted_iota(i32, table.shape, 0) == lax.broadcasted_iota(i32, table.shape, 1)
    column = jnp.sum(jnp.where(on, table, 0.0), 1, keepdims=True).astype(i32)
    chosen = column == lax.broadcasted_iota(i32, (offers, rows), 1)
    chosen = jnp.where(chosen, 1.0, 0.0).astype(bf16)
    every = jnp.concatenate([part[...] for part in ordered(latent())], 1)
    picked = matmul(chosen, every).astype(bf16)
    hidden = silu(matmul(picked, w1()[...]) + b1()[...]).astype(bf16)
    message = (matmul(hidden, w2()[...]) + b2()[...]).astype(bf16)
    for peer in range(out.shape[0]):
        out[peer] = message


def select(wanted, offered, out):
    wanted, offered = wanted(), offered()
    n_z, takes, lanes = wanted.shape
    column = 2 * n_z
    n_y = lanes // column
    offers = offered.shape[0] // (2 * n_y)
    quad = 128 // offers
    half = offered.shape[0] // 2
    shift = lax.rem(lanes - 2 * lax.axis_index("z"), lanes)
    lane = lax.broadcasted_iota(i32, (takes, 128), 1)
    blank = jnp.zeros((takes, 128), f32)
    for q in range(n_y // quad):
        sources = jnp.concatenate(
            [offered[pl.ds(c * half + q * 128, 128), :] for c in range(2)], 0
        )
        chosen = []
        for peer in range(n_z):
            table = pltpu.roll(wanted[peer], shift, 1)
            for part in range(quad):
                at = (q * quad + part) * column
                first, second = [
                    jnp.where(
                        table[:, at + c : at + c + 1] + part * offers == lane, 1.0, 0.0
                    )
                    for c in range(2)
                ]
                chosen.append(jnp.concatenate([first, blank], 1))
                chosen.append(jnp.concatenate([blank, second], 1))
        chosen = jnp.concatenate(chosen, 0).astype(bf16)
        rows = matmul(chosen, sources).astype(bf16)
        depth = quad * 2 * takes
        for peer in range(n_z):
            out[peer, pl.ds(q * depth, depth), :] = rows[peer * depth : (peer + 1) * depth]


def send(latent, w1, b1, w2, b2, node_w2, node_b2, message, side):
    rows = latent().shape[1]
    blocks = ordered(latent())
    step = rows // 2
    for r in range(0, rows, step):
        at = pl.ds(r, step)
        x = jnp.concatenate([block[at, :] for block in blocks], 1)
        hidden = silu(matmul(x, w1()[...]) + b1()[...]).astype(bf16)
        message[at, :] = (matmul(hidden, w2()[...]) + b2()[...]).astype(bf16)
    width = node_w2().shape[0]
    side[pl.ds(0, width), :] = node_w2()[...]
    row = node_b2()[...].astype(f32)
    side[pl.ds(width, TAIL), :] = jnp.broadcast_to(row, (TAIL, row.shape[1])).astype(bf16)


def above(latent, weight, side0, side1, upper, pair):
    rows = latent().shape[1]
    blocks = ordered(latent())
    step = rows // 2
    for r in range(0, rows, step):
        at = pl.ds(r, step)
        x = jnp.concatenate([block[at, :] for block in blocks], 1)
        upper[at, :] = matmul(x, weight()[...])
    pair[0] = side0()[...]
    pair[1] = side1()[...]


def tiles(source, message, halo, *rest):
    *weight, out, extended = rest
    tile, share = extended.shape[1:]
    own = message().shape[0] // tile
    for b in range(own):
        extended[b] = message()[pl.ds(b * tile, tile), :]
    peers, rows, _ = halo().shape
    run = tile // peers
    for b in range(rows // run):
        for peer in range(peers):
            extended[own + b, pl.ds(peer * run, run), :] = halo()[peer, pl.ds(b * run, run), :]
    src = source()
    group = 4
    for b, block in enumerate(weight):
        terms = block().shape[0]
        total = jnp.zeros((tile, share), f32)
        for k in range(0, terms, group):
            left = jnp.concatenate([block()[k + g] for g in range(group)], 1)
            right = jnp.concatenate([extended[src[b, k + g]] for g in range(group)], 0)
            total = total + matmul(left, right)
        out[pl.ds(b * tile, tile), :] = total.astype(bf16)


def node(lower_w, b1, *rest):
    *chunks, pair0, pair1, latent, gain, bias, out = rest
    sides = []
    r = 0
    for aggregate, upper in zip(chunks[::2], chunks[1::2]):
        parts, step, share = aggregate().shape
        width = share * parts
        at = pl.ds(r, step)
        r += step
        x = jnp.concatenate([part[...] for part in ordered(aggregate())], 1)
        hidden = silu(upper()[...] + matmul(x, lower_w()[...]) + b1()[...]).astype(bf16)
        if not sides:
            sides = [pair()[p] for pair in (pair0, pair1) for p in range(2)]
            w2 = jnp.concatenate([side[:width] for side in sides], 1)
            b2 = jnp.concatenate([side[width : width + 1] for side in sides], 1).astype(f32)
        every = matmul(hidden, w2) + b2
        split = [every[:, p * share : (p + 1) * share] for p in range(parts)]
        mine = split[0]
        total = jnp.sum(sum(split), 1, keepdims=True)
        squares = jnp.sum(sum(v * v for v in split), 1, keepdims=True)
        mean = total * (1.0 / width)
        var = squares * (1.0 / width) - mean * mean
        normed = (mine - mean) * lax.rsqrt(var + EPS)
        result = latent()[at, :].astype(f32) + gain()[...] * normed + bias()[...]
        out[at, :] = result.astype(bf16)


def local(
    latent,
    export_rows,
    halo_slots,
    tile_src,
    tile_weight,
    send_w1,
    send_b1,
    send_w2,
    send_b2,
    node_w1,
    node_b1,
    node_w2,
    node_b2,
    ln_gain,
    ln_bias,
):
    rows, share = latent.shape
    width = send_w1.shape[0]
    offers = export_rows.shape[1]
    takes = halo_slots.shape[2]
    n_y, n_z, n_core, n_sect = (lax.axis_size(name) for name in NODE + ("sect",))
    tile = tile_weight.shape[-1]
    send_b1, send_b2, node_b1, node_b2, ln_gain, ln_bias = (
        v[None] for v in (send_b1, send_b2, node_b1, node_b2, ln_gain, ln_bias)
    )

    sender = (send_w1, send_b1, send_w2, send_b2)

    slots = jnp.swapaxes(halo_slots[0], 0, 1)
    wanted = lax.all_to_all(jnp.broadcast_to(slots[None], (n_z,) + slots.shape), "z", 0, 0)
    whole = gather(latent)
    whole, wanted = lax.optimization_barrier((whole, wanted))
    (offered,) = call(
        offer, (export_rows, whole, *sender), [((n_core * n_y, offers, share), bf16)]
    )

    offered, later = lax.optimization_barrier((offered, whole))
    offered = lax.all_to_all(offered, ("core", "y"), 0, 0).reshape(-1, share)
    message, side = call(
        send,
        (later, *sender, node_w2, node_b2),
        [((rows, share), bf16), ((width + TAIL, share), bf16)],
        flops=WEIGHT,
    )
    other = lax.ppermute(side, "sect", [(i, i ^ 1) for i in range(n_sect)])
    (halo,) = call(
        select,
        (wanted, offered),
        [((n_z, n_y * n_core * takes, share), bf16)],
        flops=2 * WEIGHT,
        limit=ROOM,
    )

    halo, later = lax.optimization_barrier((halo, later))
    halo = lax.all_to_all(halo, "z", 0, 0)
    upper, pair = call(
        above,
        (later, node_w1, side, other),
        [((rows, width), f32), ((2, width + TAIL, share), bf16)],
        part={1: (pl.ds(0, width), (width, width))},
        flops=WEIGHT,
    )
    others = lax.ppermute(pair, "sect", [(i, n_sect - 1 - i) for i in range(n_sect)])

    blocks, terms = tile_src.shape
    (aggregate,) = call(
        tiles,
        (tile_src, message, halo) + (tile_weight,) * blocks,
        [((rows, share), bf16)],
        [pltpu.VMEM((rows // tile + n_y, tile, share), bf16)],
        scalars=(0,),
        part={3 + b: (b, (terms, tile, tile)) for b in range(blocks)},
        limit=ROOM,
        flops=2 * WEIGHT,
    )
    aggregate, others = gather(aggregate, others)

    step = rows // 2
    part = {0: (pl.ds(width, width), (width, width))}
    for c in range(2):
        at = pl.ds(c * step, step)
        part[2 + 2 * c] = ((slice(None), at), (n_sect, step, share))
        part[3 + 2 * c] = (at, (step, width))
    (updated,) = call(
        node,
        (node_w1, node_b1)
        + (aggregate, upper) * 2
        + (pair, others, latent, ln_gain, ln_bias),
        [((rows, share), bf16)],
        part=part,
        limit=ROOM,
    )
    return updated


def solution(mesh):
    n_mesh, n_sect = mesh.devices.shape
    n_y = n_z = int(round((n_mesh // 2) ** 0.5))
    grid = Mesh(mesh.devices.reshape(n_y, n_z, 2, n_sect), NODE + ("sect",))
    in_specs = (
        P(NODE, "sect"),
        P(NODE, None),
        P(NODE, None, None),
        P(NODE, None),
        P(NODE, None, None, None),
        P(),
        P(),
        P(None, "sect"),
        P("sect"),
        P(),
        P(),
        P(None, "sect"),
        P("sect"),
        P("sect"),
        P("sect"),
    )
    out_specs = P(NODE, "sect")
    return jax.shard_map(local, mesh=grid, in_specs=in_specs, out_specs=out_specs, check_vma=False)
```

```python
import jax
import jax.numpy as jnp
from jax import lax
from jax.experimental import pallas as pl
from jax.experimental.pallas import tpu as pltpu
from jax.sharding import Mesh
from jax.sharding import PartitionSpec as P

NODE = ("y", "z", "core")
EPS = 1e-05
TAIL = 16

LIMIT = 60 << 20
ROOM = 40 << 20
WEIGHT = 10**10
bf16, f32, i32 = jnp.bfloat16, jnp.float32, jnp.int32


def call(body, operands, outs, scratch=(), scalars=(), part={}, flops=0, limit=LIMIT):
    count = len(operands)
    moved = [i for i in range(count) if limit == LIMIT or i in scalars]
    vmem, hbm = (pl.BlockSpec(memory_space=space) for space in (pltpu.VMEM, pltpu.HBM))

    def kernel(*refs):
        sources, rest = refs[:count], refs[count:]
        results, rest = rest[: len(outs)], rest[len(outs) :]
        held, extra, sems = rest[: len(moved)], rest[len(moved) :], None
        if moved:
            extra, sems = extra[:-1], extra[-1]
        views = [ref.at[part[i][0]] if i in part else ref for i, ref in enumerate(sources)]
        copies = {
            i: pltpu.make_async_copy(views[i], held[n], sems.at[n]) for n, i in enumerate(moved)
        }
        for copy in copies.values():
            copy.start()

        def ready(i):
            def get():
                if i in copies:
                    copies.pop(i).wait()
                return held[moved.index(i)] if i in moved else views[i]

            return get

        gets = [ready(i) for i in range(count)]
        body(*gets, *results, *extra)
        for get in gets:
            get()

    scratch = list(scratch)
    if moved:
        scratch.append(pltpu.SemaphoreType.DMA((len(moved),)))
    return pl.pallas_call(
        kernel,
        out_shape=[jax.ShapeDtypeStruct(shape, kind) for shape, kind in outs],
        in_specs=[hbm if i in moved else vmem for i in range(count)],
        out_specs=[vmem] * len(outs),
        scratch_shapes=[
            (pltpu.SMEM if i in scalars else pltpu.VMEM)(
                part[i][1] if i in part else operands[i].shape, operands[i].dtype
            )
            for i in moved
        ]
        + scratch,
        compiler_params=pltpu.CompilerParams(vmem_limit_bytes=limit),
        cost_estimate=pl.CostEstimate(flops=flops, bytes_accessed=0, transcendentals=0),
        name=body.__name__,
    )(*operands)


def matmul(left, right):
    return jnp.dot(left, right, preferred_element_type=f32)


def silu(value):
    half = 0.5 * value
    return half + half * jnp.tanh(half)


def gather(block, beside=None):
    near, far = [[0, 1], [2, 3]], [[0, 3], [1, 2]]
    turned = [[0, 1], [3, 2]]
    for first, second in ((near, far), (far, turned)):
        groups = first + [[4 + i for i in group] for group in second]
        if block.ndim > 2 and beside is not None:
            block, beside = lax.optimization_barrier((block, beside))
        block = lax.all_gather(
            block, ("core", "sect"), axis=0, axis_index_groups=groups, tiled=block.ndim > 2
        )
    return block if beside is None else (block, beside)


def ordered(whole):
    core = lax.axis_index("core")
    return [whole.at[0], whole.at[1 + core], whole.at[2 + core], whole.at[3 - 2 * core]]


def spread(slots, out):
    for peer in range(out.shape[0]):
        out[peer] = slots()[...]


def offer(export, latent, w1, b1, w2, b2, out):
    rows = latent().shape[1]
    offers = out.shape[1]
    table = jnp.broadcast_to(export()[...].astype(f32), (offers, offers))
    on = lax.broadcasted_iota(i32, table.shape, 0) == lax.broadcasted_iota(i32, table.shape, 1)
    column = jnp.sum(jnp.where(on, table, 0.0), 1, keepdims=True).astype(i32)
    chosen = column == lax.broadcasted_iota(i32, (offers, rows), 1)
    chosen = jnp.where(chosen, 1.0, 0.0).astype(bf16)
    every = jnp.concatenate([part[...] for part in ordered(latent())], 1)
    picked = matmul(chosen, every).astype(bf16)
    hidden = silu(matmul(picked, w1()[...]) + b1()[...]).astype(bf16)
    message = (matmul(hidden, w2()[...]) + b2()[...]).astype(bf16)
    for peer in range(out.shape[0]):
        out[peer] = message


def select(wanted, offered, out):
    wanted, offered = wanted(), offered()
    n_z, takes, lanes = wanted.shape
    column = 2 * n_z
    n_y = lanes // column
    offers = offered.shape[0] // (2 * n_y)
    quad = 128 // offers
    half = offered.shape[0] // 2
    shift = lax.rem(lanes - 2 * lax.axis_index("z"), lanes)
    lane = lax.broadcasted_iota(i32, (takes, 128), 1)
    blank = jnp.zeros((takes, 128), f32)
    for q in range(n_y // quad):
        sources = jnp.concatenate(
            [offered[pl.ds(c * half + q * 128, 128), :] for c in range(2)], 0
        )
        chosen = []
        for peer in range(n_z):
            table = pltpu.roll(wanted[peer], shift, 1)
            for part in range(quad):
                at = (q * quad + part) * column
                first, second = [
                    jnp.where(
                        table[:, at + c : at + c + 1] + part * offers == lane, 1.0, 0.0
                    )
                    for c in range(2)
                ]
                chosen.append(jnp.concatenate([first, blank], 1))
                chosen.append(jnp.concatenate([blank, second], 1))
        chosen = jnp.concatenate(chosen, 0).astype(bf16)
        rows = matmul(chosen, sources).astype(bf16)
        depth = quad * 2 * takes
        for peer in range(n_z):
            out[peer, pl.ds(q * depth, depth), :] = rows[peer * depth : (peer + 1) * depth]


def send(latent, w1, b1, w2, b2, node_w2, node_b2, message, side):
    rows = latent().shape[1]
    blocks = ordered(latent())
    step = rows // 2
    for r in range(0, rows, step):
        at = pl.ds(r, step)
        x = jnp.concatenate([block[at, :] for block in blocks], 1)
        hidden = silu(matmul(x, w1()[...]) + b1()[...]).astype(bf16)
        message[at, :] = (matmul(hidden, w2()[...]) + b2()[...]).astype(bf16)
    width = node_w2().shape[0]
    side[pl.ds(0, width), :] = node_w2()[...]
    row = node_b2()[...].astype(f32)
    side[pl.ds(width, TAIL), :] = jnp.broadcast_to(row, (TAIL, row.shape[1])).astype(bf16)


def above(latent, weight, side0, side1, upper, pair):
    rows = latent().shape[1]
    blocks = ordered(latent())
    step = rows // 2
    for r in range(0, rows, step):
        at = pl.ds(r, step)
        x = jnp.concatenate([block[at, :] for block in blocks], 1)
        upper[at, :] = matmul(x, weight()[...])
    pair[0] = side0()[...]
    pair[1] = side1()[...]


def tiles(source, message, halo, *rest):
    *weight, out, extended = rest
    tile, share = extended.shape[1:]
    own = message().shape[0] // tile
    for b in range(own):
        extended[b] = message()[pl.ds(b * tile, tile), :]
    peers, rows, _ = halo().shape
    run = tile // peers
    for b in range(rows // run):
        for peer in range(peers):
            extended[own + b, pl.ds(peer * run, run), :] = halo()[peer, pl.ds(b * run, run), :]
    src = source()
    group = 4
    for b, block in enumerate(weight):
        terms = block().shape[0]
        total = jnp.zeros((tile, share), f32)
        for k in range(0, terms, group):
            left = jnp.concatenate([block()[k + g] for g in range(group)], 1)
            right = jnp.concatenate([extended[src[b, k + g]] for g in range(group)], 0)
            total = total + matmul(left, right)
        out[pl.ds(b * tile, tile), :] = total.astype(bf16)


def node(lower_w, b1, *rest):
    *chunks, pair0, pair1, latent, gain, bias, out = rest
    sides = []
    r = 0
    for aggregate, upper in zip(chunks[::2], chunks[1::2]):
        parts, step, share = aggregate().shape
        width = share * parts
        at = pl.ds(r, step)
        r += step
        x = jnp.concatenate([part[...] for part in ordered(aggregate())], 1)
        hidden = silu(upper()[...] + matmul(x, lower_w()[...]) + b1()[...]).astype(bf16)
        if not sides:
            sides = [pair()[p] for pair in (pair0, pair1) for p in range(2)]
            w2 = jnp.concatenate([side[:width] for side in sides], 1)
            b2 = jnp.concatenate([side[width : width + 1] for side in sides], 1).astype(f32)
        every = matmul(hidden, w2) + b2
        split = [every[:, p * share : (p + 1) * share] for p in range(parts)]
        mine = split[0]
        total = jnp.sum(sum(split), 1, keepdims=True)
        squares = jnp.sum(sum(v * v for v in split), 1, keepdims=True)
        mean = total * (1.0 / width)
        var = squares * (1.0 / width) - mean * mean
        normed = (mine - mean) * lax.rsqrt(var + EPS)
        result = latent()[at, :].astype(f32) + gain()[...] * normed + bias()[...]
        out[at, :] = result.astype(bf16)


def local(
    latent,
    export_rows,
    halo_slots,
    tile_src,
    tile_weight,
    send_w1,
    send_b1,
    send_w2,
    send_b2,
    node_w1,
    node_b1,
    node_w2,
    node_b2,
    ln_gain,
    ln_bias,
):
    rows, share = latent.shape
    width = send_w1.shape[0]
    offers = export_rows.shape[1]
    takes = halo_slots.shape[2]
    n_y, n_z, n_core, n_sect = (lax.axis_size(name) for name in NODE + ("sect",))
    tile = tile_weight.shape[-1]
    send_b1, send_b2, node_b1, node_b2, ln_gain, ln_bias = (
        v[None] for v in (send_b1, send_b2, node_b1, node_b2, ln_gain, ln_bias)
    )

    sender = (send_w1, send_b1, send_w2, send_b2)

    slots = jnp.swapaxes(halo_slots[0], 0, 1)
    (wanted,) = call(
        spread, (slots,), [((n_z,) + slots.shape, i32)], flops=WEIGHT, limit=ROOM
    )
    wanted = lax.all_to_all(wanted, "z", 0, 0)
    whole = gather(latent)
    whole, wanted = lax.optimization_barrier((whole, wanted))
    (offered,) = call(
        offer, (export_rows, whole, *sender), [((n_core * n_y, offers, share), bf16)], flops=WEIGHT, limit=ROOM
    )

    offered, later = lax.optimization_barrier((offered, whole))
    offered = lax.all_to_all(offered, ("core", "y"), 0, 0).reshape(-1, share)
    message, side = call(
        send,
        (later, *sender, node_w2, node_b2),
        [((rows, share), bf16), ((width + TAIL, share), bf16)],
        flops=WEIGHT,
        limit=ROOM,
    )
    other = lax.ppermute(side, "sect", [(i, i ^ 1) for i in range(n_sect)])
    (halo,) = call(
        select,
        (wanted, offered),
        [((n_z, n_y * n_core * takes, share), bf16)],
        flops=2 * WEIGHT,
        limit=ROOM,
    )

    halo, later = lax.optimization_barrier((halo, later))
    halo = lax.all_to_all(halo, "z", 0, 0)
    upper, pair = call(
        above,
        (later, node_w1, side, other),
        [((rows, width), f32), ((2, width + TAIL, share), bf16)],
        part={1: (pl.ds(0, width), (width, width))},
        flops=WEIGHT,
    )
    others = lax.ppermute(pair, "sect", [(i, n_sect - 1 - i) for i in range(n_sect)])

    blocks, terms = tile_src.shape
    (aggregate,) = call(
        tiles,
        (tile_src, message, halo) + (tile_weight,) * blocks,
        [((rows, share), bf16)],
        [pltpu.VMEM((rows // tile + n_y, tile, share), bf16)],
        scalars=(0,),
        part={3 + b: (b, (terms, tile, tile)) for b in range(blocks)},
        limit=ROOM,
        flops=2 * WEIGHT,
    )
    aggregate, others = gather(aggregate, others)

    step = rows // 2
    part = {0: (pl.ds(width, width), (width, width))}
    for c in range(2):
        at = pl.ds(c * step, step)
        part[2 + 2 * c] = ((slice(None), at), (n_sect, step, share))
        part[3 + 2 * c] = (at, (step, width))
    (updated,) = call(
        node,
        (node_w1, node_b1)
        + (aggregate, upper) * 2
        + (pair, others, latent, ln_gain, ln_bias),
        [((rows, share), bf16)],
        part=part,
        limit=ROOM,
    )
    return updated


def solution(mesh):
    n_mesh, n_sect = mesh.devices.shape
    n_y = n_z = int(round((n_mesh // 2) ** 0.5))
    grid = Mesh(mesh.devices.reshape(n_y, n_z, 2, n_sect), NODE + ("sect",))
    in_specs = (
        P(NODE, "sect"),
        P(NODE, None),
        P(NODE, None, None),
        P(NODE, None),
        P(NODE, None, None, None),
        P(),
        P(),
        P(None, "sect"),
        P("sect"),
        P(),
        P(),
        P(None, "sect"),
        P("sect"),
        P("sect"),
        P("sect"),
    )
    out_specs = P(NODE, "sect")
    return jax.shard_map(local, mesh=grid, in_specs=in_specs, out_specs=out_specs, check_vma=False)
```

```python
import jax
import jax.numpy as jnp
from jax import lax
from jax.experimental import pallas as pl
from jax.experimental.pallas import tpu as pltpu
from jax.sharding import Mesh
from jax.sharding import PartitionSpec as P

NODE = ("y", "z", "core")
EPS = 1e-05
TAIL = 16

LIMIT = 60 << 20
ROOM = 40 << 20
WEIGHT = 10**10
bf16, f32, i32 = jnp.bfloat16, jnp.float32, jnp.int32


def call(body, operands, outs, scratch=(), scalars=(), part={}, flops=0, limit=LIMIT):
    count = len(operands)
    moved = [i for i in range(count) if limit == LIMIT or i in scalars]
    vmem, hbm = (pl.BlockSpec(memory_space=space) for space in (pltpu.VMEM, pltpu.HBM))

    def kernel(*refs):
        sources, rest = refs[:count], refs[count:]
        results, rest = rest[: len(outs)], rest[len(outs) :]
        held, extra, sems = rest[: len(moved)], rest[len(moved) :], None
        if moved:
            extra, sems = extra[:-1], extra[-1]
        views = [ref.at[part[i][0]] if i in part else ref for i, ref in enumerate(sources)]
        copies = {
            i: pltpu.make_async_copy(views[i], held[n], sems.at[n]) for n, i in enumerate(moved)
        }
        for copy in copies.values():
            copy.start()

        def ready(i):
            def get():
                if i in copies:
                    copies.pop(i).wait()
                return held[moved.index(i)] if i in moved else views[i]

            return get

        gets = [ready(i) for i in range(count)]
        body(*gets, *results, *extra)
        for get in gets:
            get()

    scratch = list(scratch)
    if moved:
        scratch.append(pltpu.SemaphoreType.DMA((len(moved),)))
    return pl.pallas_call(
        kernel,
        out_shape=[jax.ShapeDtypeStruct(shape, kind) for shape, kind in outs],
        in_specs=[hbm if i in moved else vmem for i in range(count)],
        out_specs=[vmem] * len(outs),
        scratch_shapes=[
            (pltpu.SMEM if i in scalars else pltpu.VMEM)(
                part[i][1] if i in part else operands[i].shape, operands[i].dtype
            )
            for i in moved
        ]
        + scratch,
        compiler_params=pltpu.CompilerParams(vmem_limit_bytes=limit),
        cost_estimate=pl.CostEstimate(flops=flops, bytes_accessed=0, transcendentals=0),
        name=body.__name__,
    )(*operands)


def matmul(left, right):
    return jnp.dot(left, right, preferred_element_type=f32)


def silu(value):
    half = 0.5 * value
    return half + half * jnp.tanh(half)


def gather(block):
    near, far = [[0, 1], [2, 3]], [[0, 3], [1, 2]]
    turned = [[0, 1], [3, 2]]
    for first, second in ((near, far), (far, turned)):
        groups = first + [[4 + i for i in group] for group in second]
        block = lax.all_gather(
            block, ("core", "sect"), axis=0, axis_index_groups=groups, tiled=block.ndim > 2
        )
    return block


def ordered(whole):
    core = lax.axis_index("core")
    return [whole.at[0], whole.at[1 + core], whole.at[2 + core], whole.at[3 - 2 * core]]


def spread(slots, out):
    for peer in range(out.shape[0]):
        out[peer] = slots()[...]


def offer(export, latent, w1, b1, w2, b2, out):
    rows = latent().shape[1]
    offers = out.shape[1]
    table = jnp.broadcast_to(export()[...].astype(f32), (offers, offers))
    on = lax.broadcasted_iota(i32, table.shape, 0) == lax.broadcasted_iota(i32, table.shape, 1)
    column = jnp.sum(jnp.where(on, table, 0.0), 1, keepdims=True).astype(i32)
    chosen = column == lax.broadcasted_iota(i32, (offers, rows), 1)
    chosen = jnp.where(chosen, 1.0, 0.0).astype(bf16)
    every = jnp.concatenate([part[...] for part in ordered(latent())], 1)
    picked = matmul(chosen, every).astype(bf16)
    hidden = silu(matmul(picked, w1()[...]) + b1()[...]).astype(bf16)
    message = (matmul(hidden, w2()[...]) + b2()[...]).astype(bf16)
    for peer in range(out.shape[0]):
        out[peer] = message


def select(wanted, offered, out):
    wanted, offered = wanted(), offered()
    n_z, takes, lanes = wanted.shape
    column = 2 * n_z
    n_y = lanes // column
    offers = offered.shape[0] // (2 * n_y)
    quad = 128 // offers
    half = offered.shape[0] // 2
    shift = lax.rem(lanes - 2 * lax.axis_index("z"), lanes)
    lane = lax.broadcasted_iota(i32, (takes, 128), 1)
    blank = jnp.zeros((takes, 128), f32)
    for q in range(n_y // quad):
        sources = jnp.concatenate(
            [offered[pl.ds(c * half + q * 128, 128), :] for c in range(2)], 0
        )
        chosen = []
        for peer in range(n_z):
            table = pltpu.roll(wanted[peer], shift, 1)
            for part in range(quad):
                at = (q * quad + part) * column
                first, second = [
                    jnp.where(
                        table[:, at + c : at + c + 1] + part * offers == lane, 1.0, 0.0
                    )
                    for c in range(2)
                ]
                chosen.append(jnp.concatenate([first, blank], 1))
                chosen.append(jnp.concatenate([blank, second], 1))
        chosen = jnp.concatenate(chosen, 0).astype(bf16)
        rows = matmul(chosen, sources).astype(bf16)
        depth = quad * 2 * takes
        for peer in range(n_z):
            out[peer, pl.ds(q * depth, depth), :] = rows[peer * depth : (peer + 1) * depth]


def send(latent, w1, b1, w2, b2, node_w2, node_b2, message, side):
    rows = latent().shape[1]
    blocks = ordered(latent())
    step = rows // 2
    for r in range(0, rows, step):
        at = pl.ds(r, step)
        x = jnp.concatenate([block[at, :] for block in blocks], 1)
        hidden = silu(matmul(x, w1()[...]) + b1()[...]).astype(bf16)
        message[at, :] = (matmul(hidden, w2()[...]) + b2()[...]).astype(bf16)
    width = node_w2().shape[0]
    side[pl.ds(0, width), :] = node_w2()[...]
    row = node_b2()[...].astype(f32)
    side[pl.ds(width, TAIL), :] = jnp.broadcast_to(row, (TAIL, row.shape[1])).astype(bf16)


def above(latent, weight, upper):
    rows = latent().shape[1]
    blocks = ordered(latent())
    step = rows // 2
    for r in range(0, rows, step):
        at = pl.ds(r, step)
        x = jnp.concatenate([block[at, :] for block in blocks], 1)
        upper[at, :] = matmul(x, weight()[...])


def tiles(source, message, halo, *rest):
    *weight, out, extended = rest
    tile, share = extended.shape[1:]
    own = message().shape[0] // tile
    for b in range(own):
        extended[b] = message()[pl.ds(b * tile, tile), :]
    peers, rows, _ = halo().shape
    run = tile // peers
    for b in range(rows // run):
        for peer in range(peers):
            extended[own + b, pl.ds(peer * run, run), :] = halo()[peer, pl.ds(b * run, run), :]
    src = source()
    group = 4
    for b, block in enumerate(weight):
        terms = block().shape[0]
        total = jnp.zeros((tile, share), f32)
        for k in range(0, terms, group):
            left = jnp.concatenate([block()[k + g] for g in range(group)], 1)
            right = jnp.concatenate([extended[src[b, k + g]] for g in range(group)], 0)
            total = total + matmul(left, right)
        total = total.astype(bf16)
        for peer in range(out.shape[0]):
            out[peer, pl.ds(b * tile, tile), :] = total


def node(lower_w, b1, *rest):
    *chunks, side0, side1, side2, side3, latent, gain, bias, out = rest
    sides = []
    r = 0
    for aggregate, upper in zip(chunks[::2], chunks[1::2]):
        parts, step, share = aggregate().shape
        width = share * parts
        at = pl.ds(r, step)
        r += step
        x = jnp.concatenate([aggregate()[p] for p in range(parts)], 1)
        hidden = silu(upper()[...] + matmul(x, lower_w()[...]) + b1()[...]).astype(bf16)
        if not sides:
            sides = [side()[...] for side in (side0, side1, side2, side3)]
            w2 = jnp.concatenate([side[:width] for side in sides], 1)
            b2 = jnp.concatenate([side[width : width + 1] for side in sides], 1).astype(f32)
        every = matmul(hidden, w2) + b2
        split = [every[:, p * share : (p + 1) * share] for p in range(parts)]
        mine = split[0]
        total = jnp.sum(sum(split), 1, keepdims=True)
        squares = jnp.sum(sum(v * v for v in split), 1, keepdims=True)
        mean = total * (1.0 / width)
        var = squares * (1.0 / width) - mean * mean
        normed = (mine - mean) * lax.rsqrt(var + EPS)
        result = latent()[at, :].astype(f32) + gain()[...] * normed + bias()[...]
        out[at, :] = result.astype(bf16)


def local(
    latent,
    export_rows,
    halo_slots,
    tile_src,
    tile_weight,
    send_w1,
    send_b1,
    send_w2,
    send_b2,
    node_w1,
    node_b1,
    node_w2,
    node_b2,
    ln_gain,
    ln_bias,
):
    rows, share = latent.shape
    width = send_w1.shape[0]
    offers = export_rows.shape[1]
    takes = halo_slots.shape[2]
    n_y, n_z, n_core, n_sect = (lax.axis_size(name) for name in NODE + ("sect",))
    tile = tile_weight.shape[-1]
    send_b1, send_b2, node_b1, node_b2, ln_gain, ln_bias = (
        v[None] for v in (send_b1, send_b2, node_b1, node_b2, ln_gain, ln_bias)
    )

    sender = (send_w1, send_b1, send_w2, send_b2)

    slots = jnp.swapaxes(halo_slots[0], 0, 1)
    (wanted,) = call(
        spread, (slots,), [((n_z,) + slots.shape, i32)], flops=WEIGHT, limit=ROOM
    )
    wanted = lax.all_to_all(wanted, "z", 0, 0)
    whole = gather(latent)
    whole, wanted = lax.optimization_barrier((whole, wanted))
    (offered,) = call(
        offer, (export_rows, whole, *sender), [((n_core * n_y, offers, share), bf16)], flops=WEIGHT, limit=ROOM
    )

    offered, later = lax.optimization_barrier((offered, whole))
    offered = lax.all_to_all(offered, ("core", "y"), 0, 0).reshape(-1, share)
    message, side = call(
        send,
        (later, *sender, node_w2, node_b2),
        [((rows, share), bf16), ((width + TAIL, share), bf16)],
        flops=WEIGHT,
        limit=ROOM,
    )
    near, far = [i ^ 1 for i in range(n_sect)], [n_sect - 1 - i for i in range(n_sect)]
    first, second = (
        [(c * n_sect + i, c * n_sect + j) for c, to in enumerate(order) for i, j in enumerate(to)]
        for order in ((near, far), (far, near))
    )
    sides = [side] + [lax.ppermute(side, ("core", "sect"), to) for to in (first, second)]
    (halo,) = call(
        select,
        (wanted, offered),
        [((n_z, n_y * n_core * takes, share), bf16)],
        flops=2 * WEIGHT,
        limit=ROOM,
    )

    halo, later = lax.optimization_barrier((halo, later))
    halo = lax.all_to_all(halo, "z", 0, 0)
    later, *sides[1:] = lax.optimization_barrier((later, *sides[1:]))
    (upper,) = call(
        above,
        (later, node_w1),
        [((rows, width), f32)],
        part={1: (pl.ds(0, width), (width, width))},
        flops=WEIGHT,
    )
    passed, upper = lax.optimization_barrier((sides[1], upper))
    others = lax.ppermute(passed, ("core", "sect"), second)

    blocks, terms = tile_src.shape
    (aggregate,) = call(
        tiles,
        (tile_src, message, halo) + (tile_weight,) * blocks,
        [((n_sect, rows, share), bf16)],
        [pltpu.VMEM((rows // tile + n_y, tile, share), bf16)],
        scalars=(0,),
        part={3 + b: (b, (terms, tile, tile)) for b in range(blocks)},
        limit=ROOM,
        flops=2 * WEIGHT,
    )
    aggregate, others = lax.optimization_barrier((aggregate, others))
    aggregate = lax.all_to_all(aggregate, "sect", 0, 0)

    step = rows // 2
    part = {0: (pl.ds(width, width), (width, width))}
    for c in range(2):
        at = pl.ds(c * step, step)
        part[2 + 2 * c] = ((slice(None), at), (n_sect, step, share))
        part[3 + 2 * c] = (at, (step, width))
    (updated,) = call(
        node,
        (node_w1, node_b1)
        + (aggregate, upper) * 2
        + (*sides, others, latent, ln_gain, ln_bias),
        [((rows, share), bf16)],
        part=part,
        limit=ROOM,
    )
    return updated


def solution(mesh):
    n_mesh, n_sect = mesh.devices.shape
    n_y = n_z = int(round((n_mesh // 2) ** 0.5))
    grid = Mesh(mesh.devices.reshape(n_y, n_z, 2, n_sect), NODE + ("sect",))
    in_specs = (
        P(NODE, "sect"),
        P(NODE, None),
        P(NODE, None, None),
        P(NODE, None),
        P(NODE, None, None, None),
        P(),
        P(),
        P(None, "sect"),
        P("sect"),
        P(),
        P(),
        P(None, "sect"),
        P("sect"),
        P("sect"),
        P("sect"),
    )
    out_specs = P(NODE, "sect")
    return jax.shard_map(local, mesh=grid, in_specs=in_specs, out_specs=out_specs, check_vma=False)
```
